1024 devices in a mesh: group: 64 (over x, y), local: 16 (over z, core).
Axes of the slice: x: 8, y: 8, z: 8, core: 2. Of those that a mesh axis runs over, the one named last changes fastest.
Arguments:
- out_grad: bfloat16 [8192, 7168], P('group', 'local'), may hold values from -6 to 6
- route_groups: int32 [8192, 4], P('group'), may hold values from 0 to 63, as said below
- route_slots: int32 [8192, 4], P('group'), may hold values from 0 to 15, as said below
- route_drops: int32 [8192, 4], P('group'), may hold values 0 or 1
- combine: bfloat16 [8192, 4], P('group'), may hold values from 0.099609375 to 1
- gate_pre: bfloat16 [64, 1024, 1024], P('group'), may hold values from -8 to 8
- up_pre: bfloat16 [64, 1024, 1024], P('group'), may hold values from -6 to 6
- w_gate: bfloat16 [64, 7168, 1024], P('group', 'local'), may hold values from -0.0625 to 0.0625
- w_up: bfloat16 [64, 7168, 1024], P('group', 'local'), may hold values from -0.0625 to 0.0625
- w_down: bfloat16 [64, 1024, 7168], P('group', None, 'local'), may hold values from -0.1875 to 0.1875
Outputs:
- in_grad: bfloat16 [8192, 7168], P('group', 'local')
The draws below stay inside these ranges and needn't reach their ends.
Inputs may be any that keep to these rules, and one draw needn't show every extreme that they name: `route_groups`: each token names 4 different groups. Among the tokens of one source group (aligned blocks of 128 tokens) no group is named more than 16 times, and some group exactly 16 times in every block. `route_slots`: within one source group's tokens, the routes to one group have different slots; dropped routes have slots too.
All inputs are finite; a program needn't handle non-finite values. No bound on the sum of `route_drops` on one device may be relied on, other than what follows from the above.
Results may differ from the reference program's by a relative error of at most 0.027.
Values may be sent and summed in bfloat16 or wider, within the bound.
A program may use at most 64 MiB of HBM per device.

```python
import math
import jax
import jax.numpy as jnp
from jax import lax

D = 7168
HID = 1024
MAXG = 4
TOK_DEV = 8
CAPG = 16
SLOTS = 1024
TOKENS = 8192
N_GROUP = 64
N_LOCAL = 16


def route_tables(key):
    classes = N_GROUP // MAXG
    tokens_group = TOK_DEV * N_LOCAL

    def one_block(block_key):
        keys = jax.random.split(block_key, 5)
        order = jax.random.permutation(keys[0], N_GROUP)
        class_order = jax.random.permutation(keys[1], classes)
        tickets = class_order[jnp.arange(classes * CAPG) // CAPG]
        others = jax.random.permutation(keys[2], tickets[CAPG:])
        chosen = jnp.concatenate([tickets[:CAPG], others])[:tokens_group]
        chosen = jax.random.permutation(keys[3], chosen)
        groups = order[chosen[:, None] + classes * jnp.arange(MAXG)[None, :]]
        positions = jnp.arange(tokens_group)
        earlier = (chosen[:, None] == chosen[None, :]) & (positions[None, :] < positions[:, None])
        ranks = jnp.sum(earlier.astype(jnp.int32), axis=1)
        shuffles = jax.vmap(lambda sub_key: jax.random.permutation(sub_key, CAPG))(jax.random.split(keys[4], N_GROUP))
        slots = shuffles[groups, ranks[:, None]]
        return (groups.astype(jnp.int32), slots.astype(jnp.int32))
    groups, slots = jax.vmap(one_block)(jax.random.split(key, N_GROUP))
    return (groups.reshape(TOKENS, MAXG), slots.reshape(TOKENS, MAXG))


def draw_route_groups(key, part):
    return route_tables(key)[0]


def draw_route_slots(key, part):
    return route_tables(key)[1]


def set_ends(values, own_key, smallest, largest):
    extent = values.shape
    spot = [jax.random.randint(jax.random.fold_in(own_key, axis), (), 0, extent[axis]) for axis in range(len(extent))]
    values = values.at[tuple(spot)].set(smallest)
    longest = extent.index(max(extent))
    spot[longest] = (spot[longest] + 1) % extent[longest]
    return values.at[tuple(spot)].set(largest)


def shard_levels(stream_key, shape, shards, least, largest):
    loudness, own = 1.0, jax.random.fold_in(stream_key, 6)
    for dim, blocks in shards:
        draws = jnp.exp(jax.random.uniform(jax.random.fold_in(own, dim), (blocks,), jnp.float32, least / len(shards), largest / len(shards)))
        loudness = loudness * jnp.repeat(draws, shape[dim] // blocks).reshape([-1 if axis == dim else 1 for axis in range(len(shape))])
    return loudness


def normal_values(rng, shape, deviation, reach, cuts=(), kind=jnp.bfloat16):
    array = jax.random.normal(rng, shape, jnp.float32) * deviation
    if len(cuts) > 0:
        array = shard_levels(rng, shape, cuts, -0.22, 0.18) * array
    return jnp.clip(array, min=-reach, max=reach).astype(kind)


def setup_inputs(seed: int = 0) -> dict:
    key_of = jax.random.split(jax.random.key(seed), 11)
    out_grad = normal_values(key_of[0], (TOKENS, D), 1.0, 6.0, ((0, 64), (1, 16)))
    route_groups = draw_route_groups(jax.random.fold_in(key_of[10], 71), 0)
    route_slots = draw_route_slots(jax.random.fold_in(key_of[10], 71), 0)
    route_drops = set_ends((jax.random.randint(key_of[3], (TOKENS, MAXG), 0, 8) < 1).astype(jnp.int32), jax.random.fold_in(key_of[3], 1), 0, 1)
    combine = jnp.clip(jnp.exp(math.log(1.0) - 2.306499 * jax.random.uniform(key_of[4], (TOKENS, MAXG), jnp.float32) ** shard_levels(key_of[4], (TOKENS, MAXG), ((0, 64),), -0.2, 0.2)), 0.099609375, 1.0).astype(jnp.bfloat16)
    gate_pre = normal_values(key_of[5], (N_GROUP, HID, SLOTS), 1.5, 8.0, ((0, 64),))
    up_pre = normal_values(key_of[6], (N_GROUP, HID, SLOTS), 1.0, 6.0, ((0, 64),))
    w_gate = normal_values(key_of[7], (N_GROUP, D, HID), D ** -0.5, 0.0625, ((0, 64), (1, 16)))
    w_up = normal_values(key_of[8], (N_GROUP, D, HID), D ** -0.5, 0.0625, ((0, 64), (1, 16)))
    w_down = normal_values(key_of[9], (N_GROUP, HID, D), HID ** -0.5, 0.1875, ((0, 64), (2, 16)))
    return dict(out_grad=out_grad, route_groups=route_groups, route_slots=route_slots, route_drops=route_drops, combine=combine, gate_pre=gate_pre, up_pre=up_pre, w_gate=w_gate, w_up=w_up, w_down=w_down)


def swiglu_grad(raw_sums, gate_vals, up_vals, slot_weight):
    gate_f = gate_vals.astype(jnp.float32)
    up_f = up_vals.astype(jnp.float32)
    sigmoid_gate = jax.nn.sigmoid(gate_f)
    hidden_grad = raw_sums * slot_weight[None, :]
    gate_grad = (hidden_grad * up_f * sigmoid_gate * (1.0 + gate_f * (1.0 - sigmoid_gate))).astype(jnp.bfloat16)
    up_grad = (hidden_grad * gate_f * sigmoid_gate).astype(jnp.bfloat16)
    return (gate_grad, up_grad)

def group_grad(items):
    rows, slot_weight, gate_vals, up_vals, gate_w, up_w, down_w = items
    cols = D // N_LOCAL
    blocks = jnp.einsum('hkd,skd->khs', down_w.astype(jnp.float32).reshape(HID, N_LOCAL, cols), rows.astype(jnp.float32).reshape(SLOTS, N_LOCAL, cols))
    rounded = lax.optimization_barrier(blocks.astype(jnp.bfloat16)).astype(jnp.float32)
    raw_sums = lax.optimization_barrier(jnp.sum(rounded, axis=0))
    gate_grad, up_grad = swiglu_grad(raw_sums, gate_vals, up_vals, slot_weight)
    totals = jnp.einsum('hs,dh->sd', gate_grad.astype(jnp.float32), gate_w.astype(jnp.float32))
    totals = totals + jnp.einsum('hs,dh->sd', up_grad.astype(jnp.float32), up_w.astype(jnp.float32))
    return totals.astype(jnp.bfloat16)

def reference(out_grad, route_groups, route_slots, route_drops, combine, gate_pre, up_pre, w_gate, w_up, w_down):
    tokens_group = TOK_DEV * N_LOCAL
    source = (jnp.arange(TOKENS, dtype=jnp.int32) // tokens_group)[:, None]
    places = (source * CAPG + route_slots).astype(jnp.int32)
    kept = route_drops == 0
    route_ids = jnp.arange(TOKENS * MAXG, dtype=jnp.int32).reshape(TOKENS, MAXG)
    marked = jnp.where(kept, route_ids, -1).astype(jnp.int32)
    owner = jnp.full((N_GROUP, SLOTS), -1, jnp.int32).at[route_groups.ravel(), places.ravel()].max(marked.ravel())
    present = owner >= 0
    safe_ids = jnp.maximum(owner, 0).astype(jnp.int32)
    rows = jnp.where(present[..., None], out_grad[safe_ids // MAXG], jnp.zeros((), jnp.bfloat16)).astype(jnp.bfloat16)
    slot_weight = jnp.where(present, combine.ravel()[safe_ids].astype(jnp.float32), jnp.float32(0.0))
    slot_grad = lax.map(group_grad, (rows, slot_weight, gate_pre, up_pre, w_gate, w_up, w_down))
    gathered = slot_grad[route_groups, places].astype(jnp.float32)
    summed = lax.optimization_barrier(jnp.sum(jnp.where(kept[..., None], gathered, jnp.float32(0.0)), axis=1))
    return summed.astype(jnp.bfloat16)
```

```python
import functools
import math

import jax
import jax.numpy as jnp
from jax import lax
from jax.experimental import pallas as pl
from jax.experimental.pallas import tpu as pltpu
from jax.sharding import PartitionSpec as P

MESH = pl.DeviceIdType.MESH
F32 = jnp.float32
BF16 = jnp.bfloat16
HEAD = 16


def streams(n):
    long, short = n // 2, max(n // 2 - 1, 0)
    return ((1, 0, long), (-1, 1, long), (1, 1, short), (-1, 0, short))


def ring_gather(pos, n, device, view, send_sem, recv_sem, landed=None):
    def copy(stream, step, owner):
        sign, half, _ = streams(n)[stream]
        place = view(owner, half)
        return pltpu.make_async_remote_copy(
            src_ref=place,
            dst_ref=place,
            send_sem=send_sem.at[stream, step],
            recv_sem=recv_sem.at[stream, step],
            device_id=device(lax.rem(pos + sign + n, n)),
            device_id_type=MESH,
        )

    def owner_of(sign, step):
        return lax.rem(pos - sign * step + n, n)

    sent = []
    for step in range(n // 2 + 1):
        for stream, (sign, half, steps) in enumerate(streams(n)):
            if 0 < step <= steps:
                owner = owner_of(sign, step)
                copy(stream, step - 1, owner).wait_recv()
            if step < steps:
                going = copy(stream, step, owner_of(sign, step))
                going.start()
                sent.append(going)
            if 0 < step <= steps and landed is not None:
                landed(stream, step - 1, owner, half)
    return sent


def ring_sum(pos, n, device, term, out_buf, in_buf, send_sem, recv_sem):
    def copy(stream, step):
        sign = streams(n)[stream][0]
        return pltpu.make_async_remote_copy(
            src_ref=out_buf.at[stream, step],
            dst_ref=in_buf.at[stream, step],
            send_sem=send_sem.at[stream, step],
            recv_sem=recv_sem.at[stream, step],
            device_id=device(lax.rem(pos + sign + n, n)),
            device_id_type=MESH,
        )

    sent = []
    for step in range(n // 2):
        for stream, (sign, half, steps) in enumerate(streams(n)):
            if step >= steps:
                continue
            value = term(lax.rem(pos + sign * (steps - step) + n, n), half)
            if step > 0:
                copy(stream, step - 1).wait_recv()
                value = value + in_buf[stream, step - 1].astype(F32)
            out_buf[stream, step] = value.astype(BF16)
            going = copy(stream, step)
            going.start()
            sent.append(going)
    sums = []
    for half in range(2):
        value = term(pos, half)
        for stream, (sign, which, steps) in enumerate(streams(n)):
            if which == half and steps > 0:
                copy(stream, steps - 1).wait_recv()
                value = value + in_buf[stream, steps - 1].astype(F32)
        sums.append(value)
    return sums, sent


def kernel(
    side,
    depth,
    cap,
    ext_ref,
    gate_hbm,
    up_hbm,
    wg_hbm,
    wu_hbm,
    wd_hbm,
    out_ref,
    gate_v,
    up_v,
    wg_v,
    wu_v,
    wd_v,
    gate_f,
    up_f,
    toks,
    picks,
    order,
    msg_out,
    msg_in,
    rows,
    sib_out,
    sib_in,
    acc,
    zs_out,
    zs_in,
    raw,
    grad,
    ret_out,
    ret_in,
    part,
    fs_out,
    fs_in,
    load_sem,
    tg_send,
    tg_recv,
    a2a_send,
    a2a_recv,
    sib_send,
    sib_recv,
    zs_send,
    zs_recv,
    zg_send,
    zg_recv,
    sg_send,
    sg_recv,
    ret_send,
    ret_recv,
    fs_send,
    fs_recv,
):
    group, local = lax.axis_index("group"), lax.axis_index("local")
    core, z = lax.rem(local, 2), lax.div(local, 2)
    gx, gy = lax.div(group, side), lax.rem(group, side)
    first = gx + core * (gy - gx)
    second = gy + core * (gx - gy)
    first_step = side - core * (side - 1)
    second_step = 1 + core * (side - 1)
    sibling = (group, local + 1 - 2 * core)
    tokens = ext_ref.shape[1]
    feats = out_ref.shape[0]
    slots = gate_v.shape[1]
    hidden = gate_v.shape[0]
    block = side * cap
    half_hid = hidden // 2
    chunk = half_hid // depth
    half_slots = slots // 2

    def at_first(f):
        return (f * first_step + second * second_step, local)

    def at_second(s):
        return (first * first_step + s * second_step, local)

    def at_z(q):
        return (group, q * 2 + core)

    loads = [
        pltpu.make_async_copy(src, dst, load_sem.at[i])
        for i, (src, dst) in enumerate(
            ((gate_hbm, gate_v), (up_hbm, up_v), (wd_hbm, wd_v), (wg_hbm, wg_v), (wu_hbm, wu_v))
        )
    ]
    for load in loads:
        load.start()

    barrier = pltpu.get_barrier_semaphore()
    peers = [at_first(lax.rem(first + 1, side)), at_first(lax.rem(first + side - 1, side))]
    peers += [at_second(lax.rem(second + d, side)) for d in range(1, side)]
    if depth > 1:
        peers += [at_z(lax.rem(z + 1, depth)), at_z(lax.rem(z + depth - 1, depth))]
    peers += [sibling]
    for peer in peers:
        pl.semaphore_signal(barrier, inc=1, device_id=peer, device_id_type=MESH)
    toks[:, pl.ds(pl.multiple_of(first * tokens, tokens), tokens)] = ext_ref[...]
    picks[...] = jnp.zeros_like(picks)
    pl.semaphore_wait(barrier, len(peers))

    tok_rows = toks.shape[0]
    cut = (tok_rows // 32) * 16

    def tok_view(owner, half):
        span = pl.ds(0, cut) if half == 0 else pl.ds(cut, tok_rows - cut)
        return toks.at[span, pl.ds(pl.multiple_of(owner * tokens, tokens), tokens)]

    sent = ring_gather(first, side, at_first, tok_view, tg_send, tg_recv)

    @pl.loop(0, side)
    def _(f):
        lanes = pl.ds(pl.multiple_of(f * tokens, tokens), tokens)
        table = toks[pl.ds(feats, HEAD), lanes].astype(F32)
        place = table[4:8] * cap + table[8:12]
        slot = lax.broadcasted_iota(jnp.int32, (cap, tokens), 0)
        for e in range(side):
            wanted = ((first * first_step + e * second_step) * cap + slot).astype(F32)
            hit = wanted == place[0:1]
            for j in range(1, 4):
                hit = hit | (wanted == place[j : j + 1])
            at = pl.ds(pl.multiple_of(e * block + f * cap, cap), cap)
            picks[at, lanes] = jnp.where(hit, 1.0, 0.0).astype(BF16)

    def exchange_copy(d, out_buf, in_buf, send_sem, recv_sem):
        return pltpu.make_async_remote_copy(
            src_ref=out_buf.at[:, pl.ds(pl.multiple_of(d * block, block), block)],
            dst_ref=in_buf.at[:, pl.ds(pl.multiple_of(second * block, block), block)],
            send_sem=send_sem.at[d],
            recv_sem=recv_sem.at[d],
            device_id=at_second(lax.rem(second + d, side)),
            device_id_type=MESH,
        )

    def exchange_start(left, matrix, out_buf, in_buf, send_sem, recv_sem):
        @pl.loop(0, side)
        def _(i):
            d = lax.rem(i + side // 2, side)
            e = lax.rem(second + d, side)
            picked = matrix[pl.ds(pl.multiple_of(e * block, block), block), :]
            message = lax.dot_general(
                left[...], picked, (((1,), (1,)), ((), ())), preferred_element_type=F32
            ).astype(BF16)

            @pl.when(d == 0)
            def _():
                in_buf[:, pl.ds(pl.multiple_of(second * block, block), block)] = message

            @pl.when(d != 0)
            def _():
                out_buf[:, pl.ds(pl.multiple_of(d * block, block), block)] = message
                exchange_copy(d, out_buf, in_buf, send_sem, recv_sem).start()

    def exchange_wait(out_buf, in_buf, send_sem, recv_sem):
        @pl.loop(1, side)
        def _(d):
            exchange_copy(d, out_buf, in_buf, send_sem, recv_sem).wait()

    exchange_start(toks, picks, msg_out, msg_in, a2a_send, a2a_recv)

    loads[0].wait()
    loads[1].wait()
    strip = 16

    @pl.loop(0, hidden // strip)
    def _(i):
        at = pl.ds(pl.multiple_of(i * strip, strip), strip)
        a = gate_v[at, :].astype(F32)
        b = up_v[at, :].astype(F32)
        s = jax.nn.sigmoid(a)
        gate_f[at, :] = b * s * (1.0 + a * (1.0 - s))
        up_f[at, :] = a * s

    @pl.loop(0, side)
    def _(s):
        i = lax.broadcasted_iota(jnp.int32, (block, 1), 0)
        swapped = (i // cap) * block + s * cap + i % cap
        straight = s * block + i
        target = swapped + core * (straight - swapped)
        lane = lax.broadcasted_iota(jnp.int32, (block, slots), 1)
        order[pl.ds(pl.multiple_of(s * block, block), block), :] = jnp.where(
            lane == target, 1.0, 0.0
        ).astype(BF16)

    loads[2].wait()
    exchange_wait(msg_out, msg_in, a2a_send, a2a_recv)

    tile = min(256, slots)
    tiles = slots // tile

    @pl.loop(0, tiles)
    def _(i):
        at = pl.ds(pl.multiple_of(i * tile, tile), tile)
        rows[:, at] = jnp.dot(msg_in[...], order[:, at], preferred_element_type=F32).astype(BF16)

    def sib_copy(i):
        at = pl.ds(pl.multiple_of(i * tile, tile), tile)
        return pltpu.make_async_remote_copy(
            src_ref=sib_out.at[:, at],
            dst_ref=sib_in.at[:, at],
            send_sem=sib_send.at[i],
            recv_sem=sib_recv.at[i],
            device_id=sibling,
            device_id_type=MESH,
        )

    mine = pl.ds(pl.multiple_of(core * half_hid, half_hid), half_hid)
    other = pl.ds(pl.multiple_of((1 - core) * half_hid, half_hid), half_hid)

    @pl.loop(0, tiles)
    def _(i):
        at = pl.ds(pl.multiple_of(i * tile, tile), tile)
        sib_out[:, at] = jnp.dot(
            wd_v[other, :], rows[pl.ds(0, feats), at], preferred_element_type=F32
        ).astype(BF16)
        sib_copy(i).start()

    @pl.loop(0, tiles)
    def _(i):
        at = pl.ds(pl.multiple_of(i * tile, tile), tile)
        total = jnp.dot(wd_v[mine, :], rows[pl.ds(0, feats), at], preferred_element_type=F32)
        sib_copy(i).wait()
        acc[:, at] = total + sib_in[:, at].astype(F32)

    def z_term(owner, half):
        return acc[
            pl.ds(pl.multiple_of(owner * chunk, chunk), chunk), pl.ds(half * half_slots, half_slots)
        ]

    def raw_view(which_core, owner, half):
        at = pl.ds(pl.multiple_of(which_core * half_hid + owner * chunk, chunk), chunk)
        return raw.at[at, pl.ds(half * half_slots, half_slots)]

    sums, more = ring_sum(z, depth, at_z, z_term, zs_out, zs_in, zs_send, zs_recv)
    sent += more

    def to_sibling(which_core, owner, half, sem):
        place = raw_view(which_core, owner, half)
        return pltpu.make_async_remote_copy(
            src_ref=place,
            dst_ref=place,
            send_sem=sg_send.at[sem],
            recv_sem=sg_recv.at[sem],
            device_id=sibling,
            device_id_type=MESH,
        )

    expected = []

    def pass_on(owner, half, sem):
        going = to_sibling(core, owner, half, sem)
        going.start()
        sent.append(going)
        expected.append((owner, half, sem))

    for half in range(2):
        at = pl.ds(pl.multiple_of(core * half_hid + z * chunk, chunk), chunk)
        raw[at, pl.ds(half * half_slots, half_slots)] = sums[half].astype(BF16)

    sent += ring_gather(
        z,
        depth,
        at_z,
        lambda owner, half: raw_view(core, owner, half),
        zg_send,
        zg_recv,
        lambda stream, step, owner, half: pass_on(owner, half, 2 + stream * (depth // 2) + step),
    )
    for half in range(2):
        pass_on(z, half, half)
    for owner, half, sem in expected:
        to_sibling(1 - core, owner, half, sem).wait_recv()

    loads[3].wait()
    loads[4].wait()
    head = rows[pl.ds(feats, HEAD), :].astype(F32)
    weight = jnp.sum(
        jnp.where(head[4:8] == group.astype(F32), head[0:4], 0.0), axis=0, keepdims=True
    )
    acc[pl.ds(0, 8), :] = jnp.broadcast_to(weight, (8, slots))

    @pl.loop(0, tiles)
    def _(i):
        at = pl.ds(pl.multiple_of(i * tile, tile), tile)
        hid = raw[:, at].astype(F32) * acc[pl.ds(0, 1), at]
        gate_grad = (hid * gate_f[:, at]).astype(BF16)
        up_grad = (hid * up_f[:, at]).astype(BF16)
        total = jnp.dot(wg_v[...], gate_grad, preferred_element_type=F32)
        total = total + jnp.dot(wu_v[...], up_grad, preferred_element_type=F32)
        grad[:, at] = total.astype(BF16)

    exchange_start(grad, order, ret_out, ret_in, ret_send, ret_recv)
    exchange_wait(ret_out, ret_in, ret_send, ret_recv)

    @pl.loop(0, tiles)
    def _(i):
        at = pl.ds(pl.multiple_of(i * tile, tile), tile)
        part[:, at] = jnp.dot(ret_in[...], picks[:, at], preferred_element_type=F32)

    half_feats = feats // 2

    def tok_term(owner, half):
        return part[
            pl.ds(half * half_feats, half_feats),
            pl.ds(pl.multiple_of(owner * tokens, tokens), tokens),
        ]

    sums, more = ring_sum(first, side, at_first, tok_term, fs_out, fs_in, fs_send, fs_recv)
    sent += more
    for half in range(2):
        out_ref[pl.ds(half * half_feats, half_feats), :] = sums[half].astype(BF16)
    for going in sent:
        going.wait_send()


def shards(side, depth, out_grad, groups, slots, drops, combine, gate, up, wg, wu, wd):
    tokens, feats = out_grad.shape
    hidden, places = gate.shape[1:]
    cap = places // (side * side)
    kept = jnp.where(drops == 0, groups, -1)
    ext = jnp.concatenate(
        [
            out_grad.T,
            combine.T,
            kept.astype(BF16).T,
            slots.astype(BF16).T,
            jnp.zeros((HEAD - 12, tokens), BF16),
        ],
        axis=0,
    )
    high = feats + HEAD
    half_hid, half_feats = hidden // 2, feats // 2
    width = side * tokens
    ring, line = max(side // 2, 1), max(depth // 2, 1)
    chunk, half_places = half_hid // depth, places // 2
    tiles = places // min(256, places)
    dma = pltpu.SemaphoreType.DMA
    scratch = [
        pltpu.VMEM((hidden, places), BF16),
        pltpu.VMEM((hidden, places), BF16),
        pltpu.VMEM((feats, hidden), BF16),
        pltpu.VMEM((feats, hidden), BF16),
        pltpu.VMEM((hidden, feats), BF16),
        pltpu.VMEM((hidden, places), F32),
        pltpu.VMEM((hidden, places), F32),
        pltpu.VMEM((high, width), BF16),
        pltpu.VMEM((places, width), BF16),
        pltpu.VMEM((places, places), BF16),
        pltpu.VMEM((high, places), BF16),
        pltpu.VMEM((high, places), BF16),
        pltpu.VMEM((high, places), BF16),
        pltpu.VMEM((half_hid, places), BF16),
        pltpu.VMEM((half_hid, places), BF16),
        pltpu.VMEM((half_hid, places), F32),
        pltpu.VMEM((4, line, chunk, half_places), BF16),
        pltpu.VMEM((4, line, chunk, half_places), BF16),
        pltpu.VMEM((hidden, places), BF16),
        pltpu.VMEM((feats, places), BF16),
        pltpu.VMEM((feats, places), BF16),
        pltpu.VMEM((feats, places), BF16),
        pltpu.VMEM((feats, width), F32),
        pltpu.VMEM((4, ring, half_feats, tokens), BF16),
        pltpu.VMEM((4, ring, half_feats, tokens), BF16),
        dma((5,)),
        dma((4, ring)),
        dma((4, ring)),
        dma((side,)),
        dma((side,)),
        dma((tiles,)),
        dma((tiles,)),
        dma((4, line)),
        dma((4, line)),
        dma((4, line)),
        dma((4, line)),
        dma((2 + 4 * line,)),
        dma((2 + 4 * line,)),
        dma((side,)),
        dma((side,)),
        dma((4, ring)),
        dma((4, ring)),
    ]
    vmem, hbm = pl.BlockSpec(memory_space=pltpu.VMEM), pl.BlockSpec(memory_space=pl.ANY)
    columns = pl.pallas_call(
        functools.partial(kernel, side, depth, cap),
        out_shape=jax.ShapeDtypeStruct((feats, tokens), BF16),
        in_specs=[vmem] + [hbm] * 5,
        out_specs=vmem,
        scratch_shapes=scratch,
        compiler_params=pltpu.CompilerParams(
            collective_id=0, has_side_effects=True, vmem_limit_bytes=56 * 2**20
        ),
    )(ext, gate[0], up[0], wg[0], wu[0], wd[0])
    return columns.T


def solution(mesh):
    placed = (
        P("group", "local"),
        P("group", None),
        P("group", None),
        P("group", None),
        P("group", None),
        P("group", None, None),
        P("group", None, None),
        P("group", "local", None),
        P("group", "local", None),
        P("group", None, "local"),
    )
    side = math.isqrt(mesh.shape["group"])
    depth = mesh.shape["local"] // 2
    return jax.shard_map(
        functools.partial(shards, side, depth),
        mesh=mesh,
        in_specs=placed,
        out_specs=P("group", "local"),
        check_vma=False,
    )
```

```python
import functools
import math

import jax
import jax.numpy as jnp
from jax import lax
from jax.experimental import pallas as pl
from jax.experimental.pallas import tpu as pltpu
from jax.sharding import PartitionSpec as P

MESH = pl.DeviceIdType.MESH
F32 = jnp.float32
BF16 = jnp.bfloat16
HEAD = 16


PIECES = 4


def streams(n):
    long, short = n // 2, max(n // 2 - 1, 0)
    pairs = [(sign, piece) for piece in range(PIECES) for sign in (1, -1)]
    return [
        (sign, piece, long if (sign == 1) == (piece % 2 == 0) else short) for sign, piece in pairs
    ]


def ring_gather(pos, n, device, view, send_sem, recv_sem, landed=None):
    def copy(stream, step, owner):
        sign, piece, _ = streams(n)[stream]
        place = view(owner, piece)
        return pltpu.make_async_remote_copy(
            src_ref=place,
            dst_ref=place,
            send_sem=send_sem.at[stream, step],
            recv_sem=recv_sem.at[stream, step],
            device_id=device(lax.rem(pos + sign + n, n)),
            device_id_type=MESH,
        )

    def owner_of(sign, step):
        return lax.rem(pos - sign * step + n, n)

    sent = []
    for step in range(n // 2 + 1):
        for stream, (sign, piece, steps) in enumerate(streams(n)):
            if 0 < step <= steps:
                owner = owner_of(sign, step)
                copy(stream, step - 1, owner).wait_recv()
            if step < steps:
                going = copy(stream, step, owner_of(sign, step))
                going.start()
                sent.append(going)
            if 0 < step <= steps and landed is not None:
                landed(stream, step - 1, owner, piece)
    return sent


def ring_sum(pos, n, device, prepare, term, out_buf, in_buf, send_sem, recv_sem):
    def copy(stream, step):
        sign = streams(n)[stream][0]
        return pltpu.make_async_remote_copy(
            src_ref=out_buf.at[stream, step],
            dst_ref=in_buf.at[stream, step],
            send_sem=send_sem.at[stream, step],
            recv_sem=recv_sem.at[stream, step],
            device_id=device(lax.rem(pos + sign + n, n)),
            device_id_type=MESH,
        )

    sent = []
    for step in range(max(n // 2, 1)):
        for stream, (sign, piece, steps) in enumerate(streams(n)):
            if step == 0 and sign == 1:
                prepare(piece)
            if step >= steps:
                continue
            value = term(lax.rem(pos + sign * (steps - step) + n, n), piece)
            if step > 0:
                copy(stream, step - 1).wait_recv()
                value = value + in_buf[stream, step - 1].astype(F32)
            out_buf[stream, step] = value.astype(BF16)
            going = copy(stream, step)
            going.start()
            sent.append(going)
    sums = []
    for piece in range(PIECES):
        value = term(pos, piece)
        for stream, (sign, which, steps) in enumerate(streams(n)):
            if which == piece and steps > 0:
                copy(stream, steps - 1).wait_recv()
                value = value + in_buf[stream, steps - 1].astype(F32)
        sums.append(value)
    return sums, sent


def kernel(
    side,
    depth,
    cap,
    grad_ref,
    groups_ref,
    slots_ref,
    drops_ref,
    combine_ref,
    gate_hbm,
    up_hbm,
    wg_hbm,
    wu_hbm,
    wd_hbm,
    out_ref,
    gate_v,
    up_v,
    wg_v,
    wu_v,
    wd_soon,
    wd_late,
    wdt_v,
    gate_f,
    up_f,
    toks,
    picks,
    order,
    msg_out,
    msg_in,
    rows,
    sib_out,
    sib_in,
    acc,
    theirs,
    zs_out,
    zs_in,
    raw,
    grad,
    ret_out,
    ret_in,
    fs_out,
    fs_in,
    load_sem,
    tg_send,
    tg_recv,
    a2a_send,
    a2a_recv,
    sib_send,
    sib_recv,
    zs_send,
    zs_recv,
    zg_send,
    zg_recv,
    sg_send,
    sg_recv,
    ret_send,
    ret_recv,
    fs_send,
    fs_recv,
):
    group, local = lax.axis_index("group"), lax.axis_index("local")
    core, z = lax.rem(local, 2), lax.div(local, 2)
    gx, gy = lax.div(group, side), lax.rem(group, side)
    first = gx + core * (gy - gx)
    second = gy + core * (gx - gy)
    first_step = side - core * (side - 1)
    second_step = 1 + core * (side - 1)
    sibling = (group, local + 1 - 2 * core)
    feats, tokens = grad_ref.shape
    slots = gate_v.shape[1]
    hidden = gate_v.shape[0]
    block = side * cap
    half_hid = hidden // 2
    chunk = half_hid // depth
    span = slots // PIECES

    def at_first(f):
        return (f * first_step + second * second_step, local)

    def at_second(s):
        return (first * first_step + s * second_step, local)

    def at_z(q):
        return (group, q * 2 + core)

    loads = [
        pltpu.make_async_copy(src, dst, load_sem.at[i])
        for i, (src, dst) in enumerate(
            ((gate_hbm, gate_v), (up_hbm, up_v), (wd_hbm, wdt_v), (wg_hbm, wg_v), (wu_hbm, wu_v))
        )
    ]
    for load in loads:
        load.start()

    barrier = pltpu.get_barrier_semaphore()
    peers = [at_first(lax.rem(first + d, side)) for d in range(1, side)]
    peers += [at_second(lax.rem(second + d, side)) for d in range(1, side)]
    if depth > 1:
        peers += [at_z(lax.rem(z + 1, depth)), at_z(lax.rem(z + depth - 1, depth))]
    peers += [sibling]
    for peer in peers:
        pl.semaphore_signal(barrier, inc=1, device_id=peer, device_id_type=MESH)

    kept = jnp.where(drops_ref[...] == 0, groups_ref[...], -1).astype(F32)
    line = lax.broadcasted_iota(jnp.int32, (HEAD, tokens), 0)
    table = jnp.zeros((HEAD, tokens), F32)
    for i, values in enumerate((combine_ref[...].astype(F32), kept, slots_ref[...].astype(F32))):
        for j in range(4):
            table = jnp.where(line == 4 * i + j, values[j : j + 1], table)
    here = pl.ds(pl.multiple_of(first * tokens, tokens), tokens)
    toks[pl.ds(0, feats), here] = grad_ref[...]
    toks[pl.ds(feats, HEAD), here] = table.astype(BF16)
    pl.semaphore_wait(barrier, len(peers))

    cut = (feats // 32) * 16
    parts = (pl.ds(cut, feats - cut + HEAD), pl.ds(0, cut))
    back = (pl.ds(cut, feats - cut), pl.ds(0, cut))

    def tok_copy(d, part):
        return pltpu.make_async_remote_copy(
            src_ref=toks.at[parts[part], here],
            dst_ref=toks.at[parts[part], here],
            send_sem=tg_send.at[part, d],
            recv_sem=tg_recv.at[part, d],
            device_id=at_first(lax.rem(first + d, side)),
            device_id_type=MESH,
        )

    sent = []
    for part in range(2):
        for d in range(1, side):
            going = tok_copy(d, part)
            going.start()
            sent.append(going)
    picks[...] = jnp.zeros_like(picks)
    for d in range(1, side):
        tok_copy(d, 0).wait_recv()

    @pl.loop(0, side)
    def _(f):
        lanes = pl.ds(pl.multiple_of(f * tokens, tokens), tokens)
        table = toks[pl.ds(feats, HEAD), lanes].astype(F32)
        place = table[4:8] * cap + table[8:12]
        slot = lax.broadcasted_iota(jnp.int32, (cap, tokens), 0)
        for e in range(side):
            wanted = ((first * first_step + e * second_step) * cap + slot).astype(F32)
            hit = wanted == place[0:1]
            for j in range(1, 4):
                hit = hit | (wanted == place[j : j + 1])
            at = pl.ds(pl.multiple_of(e * block + f * cap, cap), cap)
            picks[at, lanes] = jnp.where(hit, 1.0, 0.0).astype(BF16)

    def exchange_copy(d, span, part, out_buf, in_buf, send_sem, recv_sem):
        return pltpu.make_async_remote_copy(
            src_ref=out_buf.at[span, pl.ds(pl.multiple_of(d * block, block), block)],
            dst_ref=in_buf.at[span, pl.ds(pl.multiple_of(second * block, block), block)],
            send_sem=send_sem.at[part, d],
            recv_sem=recv_sem.at[part, d],
            device_id=at_second(lax.rem(second + d, side)),
            device_id_type=MESH,
        )

    def exchange_start(left, matrix, span, part, out_buf, in_buf, send_sem, recv_sem):
        @pl.loop(0, side)
        def _(i):
            d = lax.rem(i + side // 2, side)
            e = lax.rem(second + d, side)
            picked = matrix[pl.ds(pl.multiple_of(e * block, block), block), :]
            message = lax.dot_general(
                left[span, :], picked, (((1,), (1,)), ((), ())), preferred_element_type=F32
            ).astype(BF16)

            @pl.when(d == 0)
            def _():
                in_buf[span, pl.ds(pl.multiple_of(second * block, block), block)] = message

            @pl.when(d != 0)
            def _():
                out_buf[span, pl.ds(pl.multiple_of(d * block, block), block)] = message
                exchange_copy(d, span, part, out_buf, in_buf, send_sem, recv_sem).start()

    def exchange_wait(span, part, out_buf, in_buf, send_sem, recv_sem):
        @pl.loop(1, side)
        def _(d):
            exchange_copy(d, span, part, out_buf, in_buf, send_sem, recv_sem).wait()

    exchange_start(toks, picks, parts[0], 0, msg_out, msg_in, a2a_send, a2a_recv)
    for d in range(1, side):
        tok_copy(d, 1).wait_recv()
    exchange_start(toks, picks, parts[1], 1, msg_out, msg_in, a2a_send, a2a_recv)

    loads[0].wait()
    loads[1].wait()
    strip = 16

    @pl.loop(0, hidden // strip)
    def _(i):
        at = pl.ds(pl.multiple_of(i * strip, strip), strip)
        a = gate_v[at, :].astype(F32)
        b = up_v[at, :].astype(F32)
        s = jax.nn.sigmoid(a)
        gate_f[at, :] = b * s * (1.0 + a * (1.0 - s))
        up_f[at, :] = a * s

    @pl.loop(0, side)
    def _(s):
        i = lax.broadcasted_iota(jnp.int32, (block, 1), 0)
        swapped = (i // cap) * block + s * cap + i % cap
        straight = s * block + i
        target = swapped + core * (straight - swapped)
        lane = lax.broadcasted_iota(jnp.int32, (block, slots), 1)
        order[pl.ds(pl.multiple_of(s * block, block), block), :] = jnp.where(
            lane == target, 1.0, 0.0
        ).astype(BF16)

    loads[2].wait()
    turn = min(256, hidden)
    eye = jnp.where(
        lax.broadcasted_iota(jnp.int32, (turn, turn), 0)
        == lax.broadcasted_iota(jnp.int32, (turn, turn), 1),
        1.0,
        0.0,
    ).astype(BF16)

    @pl.loop(0, hidden // turn)
    def _(i):
        at = pl.ds(pl.multiple_of(i * turn, turn), turn)
        for part in range(2):
            (wd_late, wd_soon)[1 - part][at, :] = lax.dot_general(
                eye, wdt_v[back[part], at], (((1,), (1,)), ((), ())), preferred_element_type=F32
            ).astype(BF16)

    tile = min(256, slots // PIECES)
    tiles = slots // tile
    mine = pl.ds(pl.multiple_of(core * half_hid, half_hid), half_hid)
    other = pl.ds(pl.multiple_of((1 - core) * half_hid, half_hid), half_hid)

    def sort_rows(part, at):
        rows[parts[part], at] = jnp.dot(
            msg_in[parts[part], :], order[:, at], preferred_element_type=F32
        ).astype(BF16)

    def product(part, hid, at):
        return jnp.dot(
            (wd_soon, wd_late)[part][hid, :], rows[back[part], at], preferred_element_type=F32
        )

    exchange_wait(parts[0], 0, msg_out, msg_in, a2a_send, a2a_recv)

    @pl.loop(0, tiles)
    def _(i):
        at = pl.ds(pl.multiple_of(i * tile, tile), tile)
        sort_rows(0, at)
        theirs[:, at] = product(0, other, at)
        acc[:, at] = product(0, mine, at)

    def sib_copy(i):
        at = pl.ds(pl.multiple_of(i * tile, tile), tile)
        return pltpu.make_async_remote_copy(
            src_ref=sib_out.at[:, at],
            dst_ref=sib_in.at[:, at],
            send_sem=sib_send.at[i],
            recv_sem=sib_recv.at[i],
            device_id=sibling,
            device_id_type=MESH,
        )

    exchange_wait(parts[1], 1, msg_out, msg_in, a2a_send, a2a_recv)

    @pl.loop(0, tiles)
    def _(i):
        at = pl.ds(pl.multiple_of(i * tile, tile), tile)
        sort_rows(1, at)
        sib_out[:, at] = (theirs[:, at] + product(1, other, at)).astype(BF16)
        sib_copy(i).start()

    def own_piece(piece):
        @pl.loop(piece * (tiles // PIECES), (piece + 1) * (tiles // PIECES))
        def _(i):
            at = pl.ds(pl.multiple_of(i * tile, tile), tile)
            total = acc[:, at] + product(1, mine, at)
            sib_copy(i).wait()
            acc[:, at] = total + sib_in[:, at].astype(F32)

    def z_term(owner, piece):
        return acc[
            pl.ds(pl.multiple_of(owner * chunk, chunk), chunk), pl.ds(piece * span, span)
        ]

    def raw_view(which_core, owner, piece):
        at = pl.ds(pl.multiple_of(which_core * half_hid + owner * chunk, chunk), chunk)
        return raw.at[at, pl.ds(piece * span, span)]

    sums, more = ring_sum(z, depth, at_z, own_piece, z_term, zs_out, zs_in, zs_send, zs_recv)
    sent += more

    def to_sibling(which_core, owner, piece, sem):
        place = raw_view(which_core, owner, piece)
        return pltpu.make_async_remote_copy(
            src_ref=place,
            dst_ref=place,
            send_sem=sg_send.at[sem],
            recv_sem=sg_recv.at[sem],
            device_id=sibling,
            device_id_type=MESH,
        )

    expected = []

    def pass_on(owner, piece, sem):
        going = to_sibling(core, owner, piece, sem)
        going.start()
        sent.append(going)
        expected.append((owner, piece, sem))

    for piece in range(PIECES):
        at = pl.ds(pl.multiple_of(core * half_hid + z * chunk, chunk), chunk)
        raw[at, pl.ds(piece * span, span)] = sums[piece].astype(BF16)

    sent += ring_gather(
        z,
        depth,
        at_z,
        lambda owner, piece: raw_view(core, owner, piece),
        zg_send,
        zg_recv,
        lambda stream, step, owner, piece: pass_on(owner, piece, PIECES + stream * max(depth // 2, 1) + step),
    )
    for piece in range(PIECES):
        pass_on(z, piece, piece)
    for owner, piece, sem in expected:
        to_sibling(1 - core, owner, piece, sem).wait_recv()

    loads[3].wait()
    loads[4].wait()
    head = rows[pl.ds(feats, HEAD), :].astype(F32)
    weight = jnp.sum(
        jnp.where(head[4:8] == group.astype(F32), head[0:4], 0.0), axis=0, keepdims=True
    )
    acc[pl.ds(0, 8), :] = jnp.broadcast_to(weight, (8, slots))

    def grads(part, gate_grad, up_grad):
        total = jnp.dot(wg_v[back[part], :], gate_grad, preferred_element_type=F32)
        total = total + jnp.dot(wu_v[back[part], :], up_grad, preferred_element_type=F32)
        return total.astype(BF16)

    @pl.loop(0, tiles)
    def _(i):
        at = pl.ds(pl.multiple_of(i * tile, tile), tile)
        hid = raw[:, at].astype(F32) * acc[pl.ds(0, 1), at]
        gate_grad = (hid * gate_f[:, at]).astype(BF16)
        up_grad = (hid * up_f[:, at]).astype(BF16)
        gate_v[:, at] = gate_grad
        up_v[:, at] = up_grad
        grad[back[0], at] = grads(0, gate_grad, up_grad)

    exchange_start(grad, order, back[0], 0, ret_out, ret_in, ret_send, ret_recv)

    @pl.loop(0, tiles)
    def _(i):
        at = pl.ds(pl.multiple_of(i * tile, tile), tile)
        grad[back[1], at] = grads(1, gate_v[:, at], up_v[:, at])

    exchange_start(grad, order, back[1], 1, ret_out, ret_in, ret_send, ret_recv)

    def sum_copy(d, part):
        return pltpu.make_async_remote_copy(
            src_ref=fs_out.at[back[part], pl.ds(pl.multiple_of(d * tokens, tokens), tokens)],
            dst_ref=fs_in.at[back[part], here],
            send_sem=fs_send.at[part, d],
            recv_sem=fs_recv.at[part, d],
            device_id=at_first(lax.rem(first + d, side)),
            device_id_type=MESH,
        )

    def sum_start(part):
        @pl.loop(0, side)
        def _(i):
            d = lax.rem(i + side // 2, side)
            f = lax.rem(first + d, side)
            partial = jnp.dot(
                ret_in[back[part], :],
                picks[:, pl.ds(pl.multiple_of(f * tokens, tokens), tokens)],
                preferred_element_type=F32,
            ).astype(BF16)

            @pl.when(d == 0)
            def _():
                fs_in[back[part], here] = partial

            @pl.when(d != 0)
            def _():
                fs_out[back[part], pl.ds(pl.multiple_of(d * tokens, tokens), tokens)] = partial
                sum_copy(d, part).start()

    for part in range(2):
        exchange_wait(back[part], part, ret_out, ret_in, ret_send, ret_recv)
        sum_start(part)
    for part in range(2):

        @pl.loop(1, side)
        def _(d):
            sum_copy(d, part).wait()

    total = fs_in[:, pl.ds(0, tokens)].astype(F32)
    for f in range(1, side):
        total = total + fs_in[:, pl.ds(f * tokens, tokens)].astype(F32)
    out_ref[...] = total.astype(BF16)
    for going in sent:
        going.wait_send()


def shards(side, depth, out_grad, groups, slots, drops, combine, gate, up, wg, wu, wd):
    tokens, feats = out_grad.shape
    hidden, places = gate.shape[1:]
    cap = places // (side * side)
    high = feats + HEAD
    half_hid = hidden // 2
    width = side * tokens
    line = max(depth // 2, 1)
    chunk, span = half_hid // depth, places // PIECES
    tiles = places // min(256, places // PIECES)
    dma = pltpu.SemaphoreType.DMA
    scratch = [
        pltpu.VMEM((hidden, places), BF16),
        pltpu.VMEM((hidden, places), BF16),
        pltpu.VMEM((feats, hidden), BF16),
        pltpu.VMEM((feats, hidden), BF16),
        pltpu.VMEM((hidden, feats - feats // 32 * 16), BF16),
        pltpu.VMEM((hidden, feats // 32 * 16), BF16),
        pltpu.VMEM((feats, hidden), BF16),
        pltpu.VMEM((hidden, places), F32),
        pltpu.VMEM((hidden, places), F32),
        pltpu.VMEM((high, width), BF16),
        pltpu.VMEM((places, width), BF16),
        pltpu.VMEM((places, places), BF16),
        pltpu.VMEM((high, places), BF16),
        pltpu.VMEM((high, places), BF16),
        pltpu.VMEM((high, places), BF16),
        pltpu.VMEM((half_hid, places), BF16),
        pltpu.VMEM((half_hid, places), BF16),
        pltpu.VMEM((half_hid, places), F32),
        pltpu.VMEM((half_hid, places), F32),
        pltpu.VMEM((2 * PIECES, line, chunk, span), BF16),
        pltpu.VMEM((2 * PIECES, line, chunk, span), BF16),
        pltpu.VMEM((hidden, places), BF16),
        pltpu.VMEM((feats, places), BF16),
        pltpu.VMEM((feats, places), BF16),
        pltpu.VMEM((feats, places), BF16),
        pltpu.VMEM((feats, width), BF16),
        pltpu.VMEM((feats, width), BF16),
        dma((5,)),
        dma((2, side)),
        dma((2, side)),
        dma((2, side)),
        dma((2, side)),
        dma((tiles,)),
        dma((tiles,)),
        dma((2 * PIECES, line)),
        dma((2 * PIECES, line)),
        dma((2 * PIECES, line)),
        dma((2 * PIECES, line)),
        dma((PIECES + 2 * PIECES * line,)),
        dma((PIECES + 2 * PIECES * line,)),
        dma((2, side)),
        dma((2, side)),
        dma((2, side)),
        dma((2, side)),
    ]
    vmem, hbm = pl.BlockSpec(memory_space=pltpu.VMEM), pl.BlockSpec(memory_space=pl.ANY)
    columns = pl.pallas_call(
        functools.partial(kernel, side, depth, cap),
        out_shape=jax.ShapeDtypeStruct((feats, tokens), BF16),
        in_specs=[vmem] * 5 + [hbm] * 5,
        out_specs=vmem,
        scratch_shapes=scratch,
        compiler_params=pltpu.CompilerParams(
            collective_id=0, has_side_effects=True, vmem_limit_bytes=56 * 2**20
        ),
    )(
        out_grad.T,
        groups.T,
        slots.T,
        drops.T,
        combine.T,
        gate[0],
        up[0],
        wg[0],
        wu[0],
        wd[0].T,
    )
    return columns.T


def solution(mesh):
    placed = (
        P("group", "local"),
        P("group", None),
        P("group", None),
        P("group", None),
        P("group", None),
        P("group", None, None),
        P("group", None, None),
        P("group", "local", None),
        P("group", "local", None),
        P("group", None, "local"),
    )
    side = math.isqrt(mesh.shape["group"])
    depth = mesh.shape["local"] // 2
    return jax.shard_map(
        functools.partial(shards, side, depth),
        mesh=mesh,
        in_specs=placed,
        out_specs=P("group", "local"),
        check_vma=False,
    )
```

```python
import functools
import math

import jax
import jax.numpy as jnp
from jax import lax
from jax.experimental import pallas as pl
from jax.experimental.pallas import tpu as pltpu
from jax.sharding import PartitionSpec as P

MESH = pl.DeviceIdType.MESH
F32 = jnp.float32
BF16 = jnp.bfloat16
HEAD = 16


PIECES = 4


def late_feats(feats):
    return feats // 3 // 16 * 16


def streams(n):
    long, short = n // 2, max(n // 2 - 1, 0)
    ways = [1 - 2 * (piece % 2) for piece in range(PIECES)]
    first = [(way, piece, long) for piece, way in enumerate(ways)]
    return first + [(-way, piece, short) for piece, way in enumerate(ways)]


def ring_gather(pos, n, device, view, send_sem, recv_sem, landed):
    sent = []

    def copy(stream, step, owner):
        sign, piece, _ = streams(n)[stream]
        place = view(owner, piece)
        return pltpu.make_async_remote_copy(
            src_ref=place,
            dst_ref=place,
            send_sem=send_sem.at[stream, step],
            recv_sem=recv_sem.at[stream, step],
            device_id=device(lax.rem(pos + sign + n, n)),
            device_id_type=MESH,
        )

    def owner_of(sign, step):
        return lax.rem(pos - sign * step + n, n)

    def send(stream, step, owner):
        going = copy(stream, step, owner)
        going.start()
        sent.append(going)

    def start(piece):
        for stream, (_, which, steps) in enumerate(streams(n)):
            if which == piece and steps > 0:
                send(stream, 0, pos)

    def rest():
        for step in range(1, n // 2 + 1):
            for stream, (sign, piece, steps) in enumerate(streams(n)):
                if step <= steps:
                    owner = owner_of(sign, step)
                    copy(stream, step - 1, owner).wait_recv()
                    if step < steps:
                        send(stream, step, owner)
            for offset in sorted({step, n - step}):
                landed(offset)

    return sent, start, rest


def ring_sum(pos, n, device, prepare, term, out_buf, in_buf, send_sem, recv_sem, done):
    def copy(stream, step):
        sign = streams(n)[stream][0]
        return pltpu.make_async_remote_copy(
            src_ref=out_buf.at[stream, step],
            dst_ref=in_buf.at[stream, step],
            send_sem=send_sem.at[stream, step],
            recv_sem=recv_sem.at[stream, step],
            device_id=device(lax.rem(pos + sign + n, n)),
            device_id_type=MESH,
        )

    sent = []
    for step in range(max(n // 2, 1)):
        for stream, (sign, piece, steps) in enumerate(streams(n)):
            if step == 0 and stream < PIECES:
                prepare(piece)
            if step >= steps:
                continue
            value = term(lax.rem(pos + sign * (steps - step) + n, n), piece)
            if step > 0:
                copy(stream, step - 1).wait_recv()
                value = value + in_buf[stream, step - 1].astype(F32)
            out_buf[stream, step] = value.astype(BF16)
            going = copy(stream, step)
            going.start()
            sent.append(going)
    for piece in range(PIECES):
        value = term(pos, piece)
        for stream, (sign, which, steps) in enumerate(streams(n)):
            if which == piece and steps > 0:
                copy(stream, steps - 1).wait_recv()
                value = value + in_buf[stream, steps - 1].astype(F32)
        done(piece, value)
    return sent


def kernel(
    side,
    depth,
    cap,
    grad_ref,
    groups_ref,
    slots_ref,
    drops_ref,
    combine_ref,
    gate_hbm,
    up_hbm,
    wg_hbm,
    wu_hbm,
    wd_hbm,
    out_ref,
    gate_v,
    up_v,
    wg_v,
    wu_v,
    wd_soon,
    wd_late,
    wdt_v,
    gate_f,
    up_f,
    toks,
    picks,
    order,
    msg_out,
    msg_in,
    rows,
    sib_out,
    sib_in,
    acc,
    theirs,
    zs_out,
    zs_in,
    raw,
    grad,
    ret_out,
    ret_in,
    fs_out,
    fs_in,
    out_v,
    load_sem,
    tg_send,
    tg_recv,
    a2a_send,
    a2a_recv,
    sib_send,
    sib_recv,
    zs_send,
    zs_recv,
    zg_send,
    zg_recv,
    sg_send,
    sg_recv,
    ret_send,
    ret_recv,
    fs_send,
    fs_recv,
    out_sem,
):
    group, local = lax.axis_index("group"), lax.axis_index("local")
    core, z = lax.rem(local, 2), lax.div(local, 2)
    gx, gy = lax.div(group, side), lax.rem(group, side)
    first = gx + core * (gy - gx)
    second = gy + core * (gx - gy)
    first_step = side - core * (side - 1)
    second_step = 1 + core * (side - 1)
    sibling = (group, local + 1 - 2 * core)
    feats, tokens = grad_ref.shape
    slots = gate_v.shape[1]
    hidden = gate_v.shape[0]
    block = side * cap
    half_hid = hidden // 2
    chunk = half_hid // depth
    span = slots // PIECES

    def at_first(f):
        return (f * first_step + second * second_step, local)

    def at_second(s):
        return (first * first_step + s * second_step, local)

    def at_z(q):
        return (group, q * 2 + core)

    loads = [
        pltpu.make_async_copy(src, dst, load_sem.at[i])
        for i, (src, dst) in enumerate(
            ((gate_hbm, gate_v), (up_hbm, up_v), (wd_hbm, wdt_v), (wg_hbm, wg_v), (wu_hbm, wu_v))
        )
    ]
    barrier = pltpu.get_barrier_semaphore()
    peers = [at_first(lax.rem(first + d, side)) for d in range(1, side)]
    peers += [at_second(lax.rem(second + d, side)) for d in range(1, side)]
    if depth > 1:
        peers += [at_z(lax.rem(z + 1, depth)), at_z(lax.rem(z + depth - 1, depth))]
    peers += [sibling]
    for peer in peers:
        pl.semaphore_signal(barrier, inc=1, device_id=peer, device_id_type=MESH)

    kept = jnp.where(drops_ref[...] == 0, groups_ref[...], -1).astype(F32)
    line = lax.broadcasted_iota(jnp.int32, (HEAD, tokens), 0)
    table = jnp.zeros((HEAD, tokens), F32)
    for i, values in enumerate((combine_ref[...].astype(F32), kept, slots_ref[...].astype(F32))):
        for j in range(4):
            table = jnp.where(line == 4 * i + j, values[j : j + 1], table)
    here = pl.ds(pl.multiple_of(first * tokens, tokens), tokens)
    toks[pl.ds(0, feats), here] = grad_ref[...]
    toks[pl.ds(feats, HEAD), here] = table.astype(BF16)
    pl.semaphore_wait(barrier, len(peers))

    cut = late_feats(feats)
    parts = (pl.ds(cut, feats - cut + HEAD), pl.ds(0, cut))
    back = (pl.ds(cut, feats - cut), pl.ds(0, cut))

    def tok_copy(d, part):
        return pltpu.make_async_remote_copy(
            src_ref=toks.at[parts[part], here],
            dst_ref=toks.at[parts[part], here],
            send_sem=tg_send.at[part, d],
            recv_sem=tg_recv.at[part, d],
            device_id=at_first(lax.rem(first + d, side)),
            device_id_type=MESH,
        )

    sent = []
    outward = sorted(range(1, side), key=lambda d: (abs(d - side // 2), d))
    for part in range(2):
        for d in outward:
            going = tok_copy(d, part)
            going.start()
            sent.append(going)
    for load in loads:
        load.start()
    picks[...] = jnp.zeros_like(picks)
    for d in range(1, side):
        tok_copy(d, 0).wait_recv()

    @pl.loop(0, side)
    def _(f):
        lanes = pl.ds(pl.multiple_of(f * tokens, tokens), tokens)
        table = toks[pl.ds(feats, HEAD), lanes].astype(F32)
        place = table[4:8] * cap + table[8:12]
        slot = lax.broadcasted_iota(jnp.int32, (cap, tokens), 0)
        for e in range(side):
            wanted = ((first * first_step + e * second_step) * cap + slot).astype(F32)
            hit = wanted == place[0:1]
            for j in range(1, 4):
                hit = hit | (wanted == place[j : j + 1])
            at = pl.ds(pl.multiple_of(e * block + f * cap, cap), cap)
            picks[at, lanes] = jnp.where(hit, 1.0, 0.0).astype(BF16)

    def turn_of(i):
        return side // 2 + (1 - 2 * lax.rem(i, 2)) * lax.div(i + 1, 2)

    def exchange_copy(d, span, part, out_buf, in_buf, send_sem, recv_sem):
        return pltpu.make_async_remote_copy(
            src_ref=out_buf.at[span, pl.ds(pl.multiple_of(d * block, block), block)],
            dst_ref=in_buf.at[span, pl.ds(pl.multiple_of(second * block, block), block)],
            send_sem=send_sem.at[part, d],
            recv_sem=recv_sem.at[part, d],
            device_id=at_second(lax.rem(second + d, side)),
            device_id_type=MESH,
        )

    def exchange_start(left, matrix, span, part, out_buf, in_buf, send_sem, recv_sem):
        @pl.loop(0, side)
        def _(i):
            d = turn_of(i)
            e = lax.rem(second + d, side)
            picked = matrix[pl.ds(pl.multiple_of(e * block, block), block), :]
            message = lax.dot_general(
                left[span, :], picked, (((1,), (1,)), ((), ())), preferred_element_type=F32
            ).astype(BF16)

            @pl.when(d == 0)
            def _():
                in_buf[span, pl.ds(pl.multiple_of(second * block, block), block)] = message

            @pl.when(d != 0)
            def _():
                out_buf[span, pl.ds(pl.multiple_of(d * block, block), block)] = message
                exchange_copy(d, span, part, out_buf, in_buf, send_sem, recv_sem).start()

    def exchange_wait(span, part, out_buf, in_buf, send_sem, recv_sem):
        @pl.loop(1, side)
        def _(d):
            exchange_copy(d, span, part, out_buf, in_buf, send_sem, recv_sem).wait()

    exchange_start(toks, picks, parts[0], 0, msg_out, msg_in, a2a_send, a2a_recv)
    for d in range(1, side):
        tok_copy(d, 1).wait_recv()
    exchange_start(toks, picks, parts[1], 1, msg_out, msg_in, a2a_send, a2a_recv)

    loads[0].wait()
    loads[1].wait()
    strip = 16

    @pl.loop(0, hidden // strip)
    def _(i):
        at = pl.ds(pl.multiple_of(i * strip, strip), strip)
        a = gate_v[at, :].astype(F32)
        b = up_v[at, :].astype(F32)
        s = jax.nn.sigmoid(a)
        gate_f[at, :] = b * s * (1.0 + a * (1.0 - s))
        up_f[at, :] = a * s

    @pl.loop(0, side)
    def _(s):
        i = lax.broadcasted_iota(jnp.int32, (block, 1), 0)
        swapped = (i // cap) * block + s * cap + i % cap
        straight = s * block + i
        target = swapped + core * (straight - swapped)
        lane = lax.broadcasted_iota(jnp.int32, (block, slots), 1)
        order[pl.ds(pl.multiple_of(s * block, block), block), :] = jnp.where(
            lane == target, 1.0, 0.0
        ).astype(BF16)

    loads[2].wait()
    turn = min(256, hidden)
    eye = jnp.where(
        lax.broadcasted_iota(jnp.int32, (turn, turn), 0)
        == lax.broadcasted_iota(jnp.int32, (turn, turn), 1),
        1.0,
        0.0,
    ).astype(BF16)

    @pl.loop(0, hidden // turn)
    def _(i):
        at = pl.ds(pl.multiple_of(i * turn, turn), turn)
        for part in range(2):
            (wd_late, wd_soon)[1 - part][at, :] = lax.dot_general(
                eye, wdt_v[back[part], at], (((1,), (1,)), ((), ())), preferred_element_type=F32
            ).astype(BF16)

    tile = min(256, slots // PIECES)
    tiles = slots // tile
    mine = pl.ds(pl.multiple_of(core * half_hid, half_hid), half_hid)
    other = pl.ds(pl.multiple_of((1 - core) * half_hid, half_hid), half_hid)

    def sort_rows(part, at):
        rows[parts[part], at] = jnp.dot(
            msg_in[parts[part], :], order[:, at], preferred_element_type=F32
        ).astype(BF16)

    def product(part, hid, at):
        return jnp.dot(
            (wd_soon, wd_late)[part][hid, :], rows[back[part], at], preferred_element_type=F32
        )

    exchange_wait(parts[0], 0, msg_out, msg_in, a2a_send, a2a_recv)

    @pl.loop(0, tiles)
    def _(i):
        at = pl.ds(pl.multiple_of(i * tile, tile), tile)
        sort_rows(0, at)
        theirs[:, at] = product(0, other, at)
        acc[:, at] = product(0, mine, at)

    def sib_copy(i):
        at = pl.ds(pl.multiple_of(i * tile, tile), tile)
        return pltpu.make_async_remote_copy(
            src_ref=sib_out.at[:, at],
            dst_ref=sib_in.at[:, at],
            send_sem=sib_send.at[i],
            recv_sem=sib_recv.at[i],
            device_id=sibling,
            device_id_type=MESH,
        )

    exchange_wait(parts[1], 1, msg_out, msg_in, a2a_send, a2a_recv)

    @pl.loop(0, tiles)
    def _(i):
        at = pl.ds(pl.multiple_of(i * tile, tile), tile)
        sort_rows(1, at)
        sib_out[:, at] = (theirs[:, at] + product(1, other, at)).astype(BF16)
        sib_copy(i).start()

    def own_piece(piece):
        @pl.loop(piece * (tiles // PIECES), (piece + 1) * (tiles // PIECES))
        def _(i):
            at = pl.ds(pl.multiple_of(i * tile, tile), tile)
            total = acc[:, at] + product(1, mine, at)
            sib_copy(i).wait()
            acc[:, at] = total + sib_in[:, at].astype(F32)

    def z_term(owner, piece):
        return acc[
            pl.ds(pl.multiple_of(owner * chunk, chunk), chunk), pl.ds(piece * span, span)
        ]

    def raw_view(which_core, owner, piece):
        at = pl.ds(pl.multiple_of(which_core * half_hid + owner * chunk, chunk), chunk)
        return raw.at[at, pl.ds(piece * span, span)]

    def to_sibling(which_core, offset):
        owner = lax.rem(z + offset, depth)
        at = pl.ds(pl.multiple_of(which_core * half_hid + owner * chunk, chunk), chunk)
        return pltpu.make_async_remote_copy(
            src_ref=raw.at[at, :],
            dst_ref=raw.at[at, :],
            send_sem=sg_send.at[offset],
            recv_sem=sg_recv.at[offset],
            device_id=sibling,
            device_id_type=MESH,
        )

    def pass_on(offset):
        going = to_sibling(core, offset)
        going.start()
        sent.append(going)

    gathered, gather_start, gather_rest = ring_gather(
        z, depth, at_z, lambda owner, piece: raw_view(core, owner, piece), zg_send, zg_recv, pass_on
    )

    def summed(piece, value):
        at = pl.ds(pl.multiple_of(core * half_hid + z * chunk, chunk), chunk)
        raw[at, pl.ds(piece * span, span)] = value.astype(BF16)
        gather_start(piece)
        if piece == PIECES - 1:
            pass_on(0)

    sent += ring_sum(
        z, depth, at_z, own_piece, z_term, zs_out, zs_in, zs_send, zs_recv, summed
    )
    gather_rest()
    sent += gathered
    for offset in range(depth):
        to_sibling(1 - core, offset).wait_recv()

    loads[3].wait()
    loads[4].wait()
    head = rows[pl.ds(feats, HEAD), :].astype(F32)
    weight = jnp.sum(
        jnp.where(head[4:8] == group.astype(F32), head[0:4], 0.0), axis=0, keepdims=True
    )
    acc[pl.ds(0, 8), :] = jnp.broadcast_to(weight, (8, slots))

    def grads(part, gate_grad, up_grad):
        total = jnp.dot(wg_v[back[part], :], gate_grad, preferred_element_type=F32)
        total = total + jnp.dot(wu_v[back[part], :], up_grad, preferred_element_type=F32)
        return total.astype(BF16)

    @pl.loop(0, tiles)
    def _(i):
        at = pl.ds(pl.multiple_of(i * tile, tile), tile)
        hid = raw[:, at].astype(F32) * acc[pl.ds(0, 1), at]
        gate_grad = (hid * gate_f[:, at]).astype(BF16)
        up_grad = (hid * up_f[:, at]).astype(BF16)
        gate_v[:, at] = gate_grad
        up_v[:, at] = up_grad
        grad[back[0], at] = grads(0, gate_grad, up_grad)

    exchange_start(grad, order, back[0], 0, ret_out, ret_in, ret_send, ret_recv)

    @pl.loop(0, tiles)
    def _(i):
        at = pl.ds(pl.multiple_of(i * tile, tile), tile)
        grad[back[1], at] = grads(1, gate_v[:, at], up_v[:, at])

    exchange_start(grad, order, back[1], 1, ret_out, ret_in, ret_send, ret_recv)

    def sum_copy(d, part):
        return pltpu.make_async_remote_copy(
            src_ref=fs_out.at[back[part], pl.ds(pl.multiple_of(d * tokens, tokens), tokens)],
            dst_ref=fs_in.at[back[part], here],
            send_sem=fs_send.at[part, d],
            recv_sem=fs_recv.at[part, d],
            device_id=at_first(lax.rem(first + d, side)),
            device_id_type=MESH,
        )

    def sum_start(part):
        @pl.loop(0, side)
        def _(i):
            d = turn_of(i)
            f = lax.rem(first + d, side)
            partial = jnp.dot(
                ret_in[back[part], :],
                picks[:, pl.ds(pl.multiple_of(f * tokens, tokens), tokens)],
                preferred_element_type=F32,
            ).astype(BF16)

            @pl.when(d == 0)
            def _():
                fs_in[back[part], here] = partial

            @pl.when(d != 0)
            def _():
                fs_out[back[part], pl.ds(pl.multiple_of(d * tokens, tokens), tokens)] = partial
                sum_copy(d, part).start()

    for going in sent:
        going.wait_send()
    for part in range(2):
        exchange_wait(back[part], part, ret_out, ret_in, ret_send, ret_recv)
        sum_start(part)
    def result_copy(part):
        return pltpu.make_async_copy(
            out_v.at[back[part], :], out_ref.at[back[part], :], out_sem.at[part]
        )

    for part in range(2):

        @pl.loop(1, side)
        def _(d):
            sum_copy(d, part).wait()

        total = fs_in[back[part], pl.ds(0, tokens)].astype(F32)
        for f in range(1, side):
            total = total + fs_in[back[part], pl.ds(f * tokens, tokens)].astype(F32)
        out_v[back[part], :] = total.astype(BF16)
        result_copy(part).start()
    for part in range(2):
        result_copy(part).wait()


def shards(side, depth, out_grad, groups, slots, drops, combine, gate, up, wg, wu, wd):
    tokens, feats = out_grad.shape
    hidden, places = gate.shape[1:]
    cap = places // (side * side)
    high = feats + HEAD
    half_hid = hidden // 2
    width = side * tokens
    line = max(depth // 2, 1)
    chunk, span = half_hid // depth, places // PIECES
    tiles = places // min(256, places // PIECES)
    dma = pltpu.SemaphoreType.DMA
    scratch = [
        pltpu.VMEM((hidden, places), BF16),
        pltpu.VMEM((hidden, places), BF16),
        pltpu.VMEM((feats, hidden), BF16),
        pltpu.VMEM((feats, hidden), BF16),
        pltpu.VMEM((hidden, feats - late_feats(feats)), BF16),
        pltpu.VMEM((hidden, late_feats(feats)), BF16),
        pltpu.VMEM((feats, hidden), BF16),
        pltpu.VMEM((hidden, places), F32),
        pltpu.VMEM((hidden, places), F32),
        pltpu.VMEM((high, width), BF16),
        pltpu.VMEM((places, width), BF16),
        pltpu.VMEM((places, places), BF16),
        pltpu.VMEM((high, places), BF16),
        pltpu.VMEM((high, places), BF16),
        pltpu.VMEM((high, places), BF16),
        pltpu.VMEM((half_hid, places), BF16),
        pltpu.VMEM((half_hid, places), BF16),
        pltpu.VMEM((half_hid, places), F32),
        pltpu.VMEM((half_hid, places), F32),
        pltpu.VMEM((2 * PIECES, line, chunk, span), BF16),
        pltpu.VMEM((2 * PIECES, line, chunk, span), BF16),
        pltpu.VMEM((hidden, places), BF16),
        pltpu.VMEM((feats, places), BF16),
        pltpu.VMEM((feats, places), BF16),
        pltpu.VMEM((feats, places), BF16),
        pltpu.VMEM((feats, width), BF16),
        pltpu.VMEM((feats, width), BF16),
        pltpu.VMEM((feats, tokens), BF16),
        dma((5,)),
        dma((2, side)),
        dma((2, side)),
        dma((2, side)),
        dma((2, side)),
        dma((tiles,)),
        dma((tiles,)),
        dma((2 * PIECES, line)),
        dma((2 * PIECES, line)),
        dma((2 * PIECES, line)),
        dma((2 * PIECES, line)),
        dma((depth,)),
        dma((depth,)),
        dma((2, side)),
        dma((2, side)),
        dma((2, side)),
        dma((2, side)),
        dma((2,)),
    ]
    vmem, hbm = pl.BlockSpec(memory_space=pltpu.VMEM), pl.BlockSpec(memory_space=pl.ANY)
    columns = pl.pallas_call(
        functools.partial(kernel, side, depth, cap),
        out_shape=jax.ShapeDtypeStruct((feats, tokens), BF16),
        in_specs=[vmem] * 5 + [hbm] * 5,
        out_specs=hbm,
        scratch_shapes=scratch,
        compiler_params=pltpu.CompilerParams(
            collective_id=0, has_side_effects=True, vmem_limit_bytes=56 * 2**20
        ),
    )(
        out_grad.T,
        groups.T,
        slots.T,
        drops.T,
        combine.T,
        gate[0],
        up[0],
        wg[0],
        wu[0],
        wd[0].T,
    )
    return columns.T


def solution(mesh):
    placed = (
        P("group", "local"),
        P("group", None),
        P("group", None),
        P("group", None),
        P("group", None),
        P("group", None, None),
        P("group", None, None),
        P("group", "local", None),
        P("group", "local", None),
        P("group", None, "local"),
    )
    side = math.isqrt(mesh.shape["group"])
    depth = mesh.shape["local"] // 2
    return jax.shard_map(
        functools.partial(shards, side, depth),
        mesh=mesh,
        in_specs=placed,
        out_specs=P("group", "local"),
        check_vma=False,
    )
```
